256 devices in a mesh: prompt: 32 (over x_lo, z, core), tensor: 8 (over x_hi, y).
Axes of the slice: x: 4 (x_hi: 2, x_lo: 2; x = x_hi * 2 + x_lo), y: 4, z: 8, core: 2. Of those that a mesh axis runs over, the one named last changes fastest.
Arguments:
- state_hidden: bfloat16 [64, 128, 4096], P('prompt', None, 'tensor'), may hold values from -12 to 12
- prefix_hidden: bfloat16 [32, 1024, 4096], P('prompt', None, 'tensor'), may hold values from -12 to 12
- norm_gain: bfloat16 [4096], replicated, may hold values from 0.099609375 to 1.8984375
- w_query: bfloat16 [4096, 4096], P(None, 'tensor'), may hold values from -1 to 1
- w_key: bfloat16 [4096, 1024], P(None, 'tensor'), may hold values from -1 to 1
- w_value: bfloat16 [4096, 1024], P(None, 'tensor'), may hold values from -0.09375 to 0.09375
- w_out: bfloat16 [4096, 4096], P('tensor'), may hold values from -0.09375 to 0.09375
- scored_prompt: int32 [32, 2], P('prompt'), may hold values from 0 to 31, as said below
- prefix_len: int32 [32], replicated, may hold values from 1 to 1024, as said below
- state_mask: int32 [64, 128], P('prompt'), may hold values 0 or 1
Outputs:
- mixed: bfloat16 [64, 128, 4096], P('prompt', None, 'tensor')
The draws below stay inside these ranges and needn't reach their ends.
Inputs may be any that keep to these rules, and one draw needn't show every extreme that they name: `scored_prompt`: each column is a permutation of the prompts, so every prompt has exactly 2 states, one in each slot. `prefix_len`: some prompt uses all 1024 positions.
All inputs are finite; a program needn't handle non-finite values. No bound on the sum of `state_mask` on one device may be relied on, other than what follows from the above.
Results may differ from the reference program's by a relative error of at most 0.017.
Values may be sent and summed in bfloat16 or wider, within the bound.
No kernel may reach another device: no remote copies, remote signals or barrier semaphores. Data moves between devices by JAX's collectives and lax.ppermute only.
A program may use at most 128 MiB of HBM per device.

```python
import math
import jax
import jax.numpy as jnp
from jax import lax

D = 4096
HEADS = 32
KV_HEADS = 8
HEAD_DIM = 128
PREFIX = 1024
STATE_LEN = 128
SPP = 2
PROMPTS = 32
STATES = 64
N_TENSOR = 8


def spike_signs(key):
    flips = jax.random.bernoulli(jax.random.fold_in(key, 101), 0.5, (D,))
    return jnp.where(flips, 1.0, -1.0).astype(jnp.float32)


def spike_rows(key):
    return jax.random.truncated_normal(jax.random.fold_in(key, 102), -3.0, 3.0, (KV_HEADS, HEAD_DIM), jnp.float32)


def place_spikes(key, base, signs, share):
    first, second = jax.random.split(key)
    shape = base.shape[:-1] + (1,)
    spiky = jax.random.bernoulli(first, share, shape)
    amount = jax.random.uniform(second, shape, jnp.float32, 1.5, 6.0)
    return base + jnp.where(spiky, amount, 0.0) * signs


def draw_state_hidden(key, part):
    signs = spike_signs(key)
    key = jax.random.fold_in(key, 31)
    base_key = jax.random.fold_in(key, 0)
    spike_key = jax.random.fold_in(key, 2)
    shape = (STATES, STATE_LEN, D)
    base = jax.random.truncated_normal(base_key, -4.0, 4.0, shape, jnp.float32)
    return place_spikes(spike_key, base, signs, 1.0 / 16.0).astype(jnp.bfloat16)


def draw_prefix_hidden(key, part):
    signs = spike_signs(key)
    key = jax.random.fold_in(key, 33)
    base_key = jax.random.fold_in(key, 0)
    spike_key = jax.random.fold_in(key, 2)
    shape = (PROMPTS, PREFIX, D)
    base = jax.random.truncated_normal(base_key, -4.0, 4.0, shape, jnp.float32)
    return place_spikes(spike_key, base, signs, 1.0 / 32.0).astype(jnp.bfloat16)


def draw_w_query(key, part):
    signs = spike_signs(key)
    pattern_rows = spike_rows(key)
    key = jax.random.fold_in(key, 37)
    base_key, strength_key = jax.random.split(key)
    base = jax.random.truncated_normal(base_key, -4.0, 4.0, (D, HEADS * HEAD_DIM), jnp.float32) * D ** (-0.5)
    strength = jnp.exp(jax.random.uniform(strength_key, (HEADS, 1), jnp.float32, math.log(3.0), math.log(10.0)))
    pattern = (jnp.repeat(pattern_rows, HEADS // KV_HEADS, axis=0) * strength).reshape(HEADS * HEAD_DIM)
    return (base + signs[:, None] * pattern[None, :] / D).astype(jnp.bfloat16)


def draw_w_key(key, part):
    signs = spike_signs(key)
    pattern_rows = spike_rows(key)
    key = jax.random.fold_in(key, 41)
    base = jax.random.truncated_normal(key, -4.0, 4.0, (D, KV_HEADS * HEAD_DIM), jnp.float32) * D ** (-0.5)
    pattern = (4.0 * pattern_rows).reshape(KV_HEADS * HEAD_DIM)
    return (base + signs[:, None] * pattern[None, :] / D).astype(jnp.bfloat16)


def draw_scored_prompt(key, part):
    key = jax.random.fold_in(key, 11)
    columns = [jax.random.permutation(jax.random.fold_in(key, slot), PROMPTS) for slot in range(SPP)]
    return jnp.stack(columns, axis=1).astype(jnp.int32)


def draw_prefix_len(key, part):
    key = jax.random.fold_in(key, 23)
    first, second = jax.random.split(key)
    lengths = jax.random.randint(first, (PROMPTS,), 1, PREFIX + 1)
    longest = jax.random.randint(second, (), 0, PROMPTS)
    return jnp.where(jnp.arange(PROMPTS) == longest, PREFIX, lengths).astype(jnp.int32)


def place_ends(result, rng, low, top_value):
    longest = result.shape.index(max(result.shape))
    spots = []
    for shift in (0, 1):
        where = [jax.random.randint(jax.random.fold_in(rng, axis), (), 0, length) for axis, length in enumerate(result.shape)]
        where[longest] = (where[longest] + shift) % result.shape[longest]
        spots.append(tuple(where))
    return result.at[spots[0]].set(low).at[spots[1]].set(top_value)


def block_levels(stream_key, extent, cuts, smallest, largest):
    def one(axis_at, parts):
        heights = jax.random.uniform(jax.random.fold_in(jax.random.fold_in(stream_key, 6), axis_at), (parts,), jnp.float32, smallest / len(cuts), largest / len(cuts))
        return jnp.repeat(jnp.exp(heights), extent[axis_at] // parts).reshape((-1,) + (1,) * (len(extent) - axis_at - 1))

    level = one(*cuts[0])
    for cut in cuts[1:]:
        level = level * one(*cut)
    return level


def gaussian(key, shape, scale, most, cuts=(), held_as=jnp.bfloat16):
    level = block_levels(key, shape, cuts, -0.22, 0.18) if cuts else 1.0
    values = jax.random.normal(key, shape, jnp.float32) * scale * level
    return jnp.minimum(jnp.maximum(values, -most), most).astype(held_as)


def setup_inputs(seed: int = 0) -> dict:
    seeds = jax.random.split(jax.random.key(seed), 11)
    state_hidden = draw_state_hidden(jax.random.fold_in(seeds[10], 71), 0)
    prefix_hidden = draw_prefix_hidden(jax.random.fold_in(seeds[10], 71), 0)
    norm_gain = jnp.clip(1.0 + 0.18 * jax.random.normal(seeds[2], (D,), jnp.float32), 0.099609375, 1.8984375).astype(jnp.bfloat16)
    w_query = draw_w_query(jax.random.fold_in(seeds[10], 71), 0)
    w_key = draw_w_key(jax.random.fold_in(seeds[10], 71), 0)
    w_value = gaussian(seeds[5], (D, KV_HEADS * HEAD_DIM), D ** -0.5, 0.09375, ((1, 8),))
    w_out = gaussian(seeds[6], (HEADS * HEAD_DIM, D), (HEADS * HEAD_DIM) ** -0.5, 0.09375, ((0, 8),))
    scored_prompt = draw_scored_prompt(jax.random.fold_in(seeds[10], 71), 0)
    prefix_len = draw_prefix_len(jax.random.fold_in(seeds[10], 71), 0)
    state_mask = place_ends((jax.random.randint(seeds[9], (STATES, STATE_LEN), 0, 8) < 7).astype(jnp.int32), jax.random.fold_in(seeds[9], 1), 0, 1)
    return dict(state_hidden=state_hidden, prefix_hidden=prefix_hidden, norm_gain=norm_gain, w_query=w_query, w_key=w_key, w_value=w_value, w_out=w_out, scored_prompt=scored_prompt, prefix_len=prefix_len, state_mask=state_mask)


def normalize(hidden, gain):
    values = hidden.astype(jnp.float32)
    scale = lax.rsqrt(lax.optimization_barrier(jnp.mean(values * values, axis=-1, keepdims=True)) + 1e-05)
    return (values * scale * gain.astype(jnp.float32)).astype(jnp.bfloat16)

def reference(state_hidden, prefix_hidden, norm_gain, w_query, w_key, w_value, w_out, scored_prompt, prefix_len, state_mask):
    group = HEADS // KV_HEADS
    normed_state = normalize(state_hidden, norm_gain).reshape(-1, D)
    normed_prefix = normalize(prefix_hidden, norm_gain).reshape(-1, D)
    prefix_keys = jnp.dot(normed_prefix, w_key, preferred_element_type=jnp.float32).astype(jnp.bfloat16).reshape(PROMPTS, PREFIX, KV_HEADS, HEAD_DIM)
    prefix_values = jnp.dot(normed_prefix, w_value, preferred_element_type=jnp.float32).astype(jnp.bfloat16).reshape(PROMPTS, PREFIX, KV_HEADS, HEAD_DIM)
    queries = (jnp.dot(normed_state, w_query, preferred_element_type=jnp.float32) * HEAD_DIM ** (-0.5)).astype(jnp.bfloat16)
    queries = queries.reshape(STATES, STATE_LEN, KV_HEADS, group, HEAD_DIM)
    state_keys = jnp.dot(normed_state, w_key, preferred_element_type=jnp.float32).astype(jnp.bfloat16).reshape(STATES, STATE_LEN, KV_HEADS, HEAD_DIM)
    state_values = jnp.dot(normed_state, w_value, preferred_element_type=jnp.float32).astype(jnp.bfloat16).reshape(STATES, STATE_LEN, KV_HEADS, HEAD_DIM)
    owners = scored_prompt.reshape(-1).astype(jnp.int32)
    positions = jnp.arange(PREFIX, dtype=jnp.int32)
    tokens = jnp.arange(STATE_LEN, dtype=jnp.int32)

    def attend_state(items):
        query, keys_own, values_own, owner, mask_row = items
        keys = jnp.concatenate([prefix_keys[owner], keys_own], axis=0).astype(jnp.float32)
        values = jnp.concatenate([prefix_values[owner], values_own], axis=0).astype(jnp.float32)
        scores = jnp.einsum('tkgd,jkd->kgtj', query.astype(jnp.float32), keys)
        valid_prefix = jnp.broadcast_to((positions < prefix_len[owner])[None, :], (STATE_LEN, PREFIX))
        causal = (tokens[None, :] <= tokens[:, None]) & (mask_row[None, :] == 1)
        valid = jnp.concatenate([valid_prefix, causal], axis=1)
        scores = jnp.where(valid, scores, -1e+30)
        top = lax.optimization_barrier(jnp.max(scores, axis=-1, keepdims=True))
        weights = jnp.where(valid, jnp.exp(scores - top), 0.0)
        numer = jnp.einsum('kgtj,jkd->tkgd', weights.astype(jnp.bfloat16).astype(jnp.float32), values)
        denom = jnp.transpose(lax.optimization_barrier(jnp.sum(weights, axis=-1)), (2, 0, 1))[..., None]
        return (numer / denom).astype(jnp.bfloat16).reshape(STATE_LEN, HEADS * HEAD_DIM)
    attended = lax.map(attend_state, (queries, state_keys, state_values, owners, state_mask))
    flat = attended.reshape(-1, HEADS * HEAD_DIM)
    width = HEADS * HEAD_DIM // N_TENSOR
    total = jnp.zeros((flat.shape[0], D), jnp.float32)
    for shard in range(N_TENSOR):
        piece = jnp.dot(flat[:, shard * width:(shard + 1) * width], w_out[shard * width:(shard + 1) * width], preferred_element_type=jnp.float32)
        rounded = lax.optimization_barrier(piece.astype(jnp.bfloat16))
        total = total + rounded.astype(jnp.float32)
    return total.astype(jnp.bfloat16).reshape(STATES, STATE_LEN, D)
```

```python
import functools

import jax
import jax.numpy as jnp
from jax import lax
from jax.experimental import pallas as pl
from jax.experimental.pallas import tpu as pltpu
from jax.sharding import Mesh, PartitionSpec as P

HEAD_DIM = 128
CHIPS = ("xl", "z")
TENSOR = ("xh", "y")
PROMPT = ("xl", "z", "c")
F32 = jnp.float32
BF16 = jnp.bfloat16


def vmem():
    return pl.BlockSpec(memory_space=pltpu.VMEM)


def smem():
    return pl.BlockSpec(memory_space=pltpu.SMEM)


def params(mib):
    return pltpu.CompilerParams(vmem_limit_bytes=mib << 20)


def inverse_rms(total, width):
    return lax.rsqrt(total / width + 1e-05)


def dot(a, b):
    return jnp.dot(a, b, preferred_element_type=F32)


def dot_t(a, b):
    return lax.dot_general(a, b, (((1,), (1,)), ((), ())), preferred_element_type=F32)


def prefix_kernel(where, gain, *refs):
    blocks, (w_k, w_v, w_a, w_b, own, back, acc) = refs[:8], refs[8:]
    xh, y, c = where[0], where[1], where[2]
    rows, part = blocks[0].shape
    tile = 256

    def step(r, carry):
        at = pl.ds(pl.multiple_of(r * tile, tile), tile)
        total = jnp.zeros((tile, 1), F32)
        for block in blocks:
            x = block[at, :].astype(F32)
            total += jnp.sum(x * x, axis=1, keepdims=True)
        scale = inverse_rms(total, 8 * part)
        for k, block in enumerate(blocks):
            half = xh if k < 4 else 1 - xh
            feature = half * 4 + ((y + 4 - k % 4) & 3)
            g = gain[feature].astype(F32)
            n = (block[at, :].astype(F32) * scale * g).astype(BF16)
            wat = pl.ds(pl.multiple_of(feature * part, part), part)
            w = jnp.concatenate([w_k[wat, :], w_v[wat, :], w_a[wat, :], w_b[wat, :]], axis=1)
            if k == 0:
                acc[...] = dot(n, w)
            else:
                acc[...] += dot(n, w)
        own[at, :] = acc[:, : 2 * HEAD_DIM].astype(BF16)
        a = acc[:, 2 * HEAD_DIM : 3 * HEAD_DIM]
        b = acc[:, 3 * HEAD_DIM :]
        back[at, :HEAD_DIM] = jnp.where(c == 0, a, b).astype(BF16)
        back[at, HEAD_DIM:] = jnp.where(c == 0, b, a).astype(BF16)
        return carry

    lax.fori_loop(0, rows // tile, step, 0)


def state_kernel(x, gain, w_q, w_k, w_v, q, k, v, acc):
    parts, rows, part = x.shape
    total = jnp.zeros((rows, 1), F32)
    for f in range(parts):
        h = x[f].astype(F32)
        total += jnp.sum(h * h, axis=1, keepdims=True)
    scale = inverse_rms(total, parts * part)
    for f in range(parts):
        n = (x[f].astype(F32) * scale * gain[f].astype(F32)).astype(BF16)
        at = slice(f * part, (f + 1) * part)
        w = jnp.concatenate([w_q[at, :], w_k[at, :], w_v[at, :]], axis=1)
        if f == 0:
            acc[...] = dot(n, w)
        else:
            acc[...] += dot(n, w)
    split = w_q.shape[1]
    q[...] = (acc[:, :split] * HEAD_DIM ** (-0.5)).astype(BF16)
    k[...] = acc[:, split : split + HEAD_DIM].astype(BF16)
    v[...] = acc[:, split + HEAD_DIM :].astype(BF16)


def attention_kernel(where, q, near, far, k, v, meta, w_out, out, att):
    xh, limit = where[0], where[1]
    rows = q.shape[0]
    half = near.shape[0]
    column = lax.broadcasted_iota(jnp.int32, (1, half), 1)
    near_ok = xh * half + column < limit
    far_ok = (1 - xh) * half + column < limit
    pick = (lax.broadcasted_iota(jnp.int32, (8, HEAD_DIM), 1) == 1).astype(BF16)
    present = dot_t(pick, meta[...])[0:1, :] > 0.5
    a = lax.broadcasted_iota(jnp.int32, (rows, rows), 0)
    b = lax.broadcasted_iota(jnp.int32, (rows, rows), 1)
    same = ((a >> 3) & 1) == ((b >> 3) & 1)
    before = (((b >> 4) << 3) | (b & 7)) <= (((a >> 4) << 3) | (a & 7))
    own_ok = same & before & present
    k_near, v_near = near[:, :HEAD_DIM], near[:, HEAD_DIM:]
    k_far, v_far = far[:, :HEAD_DIM], far[:, HEAD_DIM:]
    for h in range(q.shape[1] // HEAD_DIM):
        at = slice(h * HEAD_DIM, (h + 1) * HEAD_DIM)
        qh = q[:, at]
        s0 = jnp.where(near_ok, dot_t(qh, k_near), -1e30)
        s1 = jnp.where(far_ok, dot_t(qh, k_far), -1e30)
        s2 = jnp.where(own_ok, dot_t(qh, k[...]), -1e30)
        top = jnp.maximum(
            jnp.maximum(jnp.max(s0, axis=1, keepdims=True), jnp.max(s1, axis=1, keepdims=True)),
            jnp.max(s2, axis=1, keepdims=True),
        )
        p0 = jnp.where(near_ok, jnp.exp(s0 - top), 0.0)
        p1 = jnp.where(far_ok, jnp.exp(s1 - top), 0.0)
        p2 = jnp.where(own_ok, jnp.exp(s2 - top), 0.0)
        denom = (
            jnp.sum(p0, axis=1, keepdims=True)
            + jnp.sum(p1, axis=1, keepdims=True)
            + jnp.sum(p2, axis=1, keepdims=True)
        )
        numer = dot(p0.astype(BF16), v_near) + dot(p1.astype(BF16), v_far)
        numer += dot(p2.astype(BF16), v[...])
        att[:, at] = (numer / denom).astype(BF16)
    part = out.shape[2]

    def project(t, carry):
        at = pl.ds(pl.multiple_of(t * part, part), part)
        out[t] = dot(att[...], w_out[:, at]).astype(BF16)
        return carry

    lax.fori_loop(0, out.shape[0], project, 0)


def select_kernel(index, own, other, out):
    chips, slots = out.shape[:2]
    for q in range(chips):
        for s in range(slots):
            j = index[q, s]
            at = j & (chips - 1)
            out[q, s] = jnp.where(j < chips, own[at, s], other[at, s])


def select(index, own, other):
    return pl.pallas_call(
        select_kernel,
        out_shape=jax.ShapeDtypeStruct(own.shape, own.dtype),
        in_specs=[smem(), vmem(), vmem()],
        out_specs=vmem(),
        compiler_params=params(16),
        cost_estimate=pl.CostEstimate(flops=0, bytes_accessed=3 * own.size * 2, transcendentals=0),
        name="select_blocks",
    )(index, own, other)


def swap(x, axis):
    return lax.ppermute(x, axis, [(0, 1), (1, 0)])


def turn(x, s):
    return lax.ppermute(x, "y", [(i, (i + s) % 4) for i in range(4)])


def spread(x, axis):
    return lax.all_to_all(x, axis, 0, 0, tiled=True)


def per_device(
    state_hidden,
    prefix_hidden,
    norm_gain,
    w_query,
    w_key,
    w_value,
    w_out,
    scored_prompt,
    prefix_len,
    state_mask,
):
    xl, z, c = lax.axis_index("xl"), lax.axis_index("z"), lax.axis_index("c")
    xh, y = lax.axis_index("xh"), lax.axis_index("y")
    slots, length, part = state_hidden.shape
    parts = 8
    chips = 16
    piece = length // chips
    rows = slots * length
    half = prefix_hidden.shape[1] // 2
    gain = norm_gain.reshape(parts, 1, part)

    mine = lax.dynamic_slice_in_dim(prefix_hidden[0], xh * half, half)
    send = lax.dynamic_slice_in_dim(prefix_hidden[0], (1 - xh) * half, half)
    got = swap(send, "xh")
    w_a = swap(jnp.where(c == 0, w_key, w_value), "xh")
    w_b = swap(w_a, "c")
    blocks = [mine] + [turn(mine, s) for s in (1, 2, 3)]
    blocks += [got] + [turn(got, s) for s in (1, 2, 3)]

    lane = lax.broadcasted_iota(jnp.int32, (slots, length, HEAD_DIM), 2)
    meta = jnp.where(lane == 0, scored_prompt[0][:, None, None], state_mask[:, :, None])
    meta = jnp.where(lane < 2, meta, 0).astype(BF16)
    packed = jnp.concatenate([state_hidden, meta], axis=2)
    packed = packed.reshape(slots, chips, piece, part + HEAD_DIM).transpose(1, 0, 2, 3)
    here = spread(packed, CHIPS)
    there = swap(here, "c")
    ids = here[:, :, 0, part].astype(jnp.int32)
    ids_there = there[:, :, 0, part].astype(jnp.int32)
    chip = jnp.arange(chips, dtype=jnp.int32)
    wanted = (2 * chip + c)[:, None, None]
    inward = jnp.sum(
        jnp.where(ids[None] == wanted, chip[None, :, None], 0)
        + jnp.where(ids_there[None] == wanted, chips + chip[None, :, None], 0),
        axis=1,
    ).astype(jnp.int32)
    outward = jnp.where(ids % 2 == c, ids // 2, chips + ids // 2)
    routed = spread(select(inward, here, there), CHIPS).reshape(rows, part + HEAD_DIM)

    wide = jnp.broadcast_to(routed[None, :, :part], (parts, rows, part))
    wide = spread(wide, TENSOR)
    q, k, v = pl.pallas_call(
        state_kernel,
        out_shape=[
            jax.ShapeDtypeStruct((rows, w_query.shape[1]), BF16),
            jax.ShapeDtypeStruct((rows, HEAD_DIM), BF16),
            jax.ShapeDtypeStruct((rows, HEAD_DIM), BF16),
        ],
        in_specs=[vmem()] * 5,
        out_specs=[vmem()] * 3,
        scratch_shapes=[pltpu.VMEM((rows, w_query.shape[1] + 2 * HEAD_DIM), F32)],
        compiler_params=params(24),
        cost_estimate=pl.CostEstimate(flops=1610612736, bytes_accessed=8 << 20, transcendentals=0),
        name="state_projection",
    )(wide, gain, w_query, w_key, w_value)

    place = jnp.stack([xh, y, c]).astype(jnp.int32)
    near, back = pl.pallas_call(
        prefix_kernel,
        out_shape=[jax.ShapeDtypeStruct((half, 2 * HEAD_DIM), BF16)] * 2,
        in_specs=[smem()] + [vmem()] * 13,
        out_specs=[vmem()] * 2,
        scratch_shapes=[pltpu.VMEM((256, 4 * HEAD_DIM), F32)],
        compiler_params=params(24),
        cost_estimate=pl.CostEstimate(flops=2147483648, bytes_accessed=8 << 20, transcendentals=0),
        name="prefix_projection",
    )(place, gain, *blocks, w_key, w_value, w_a, w_b)
    far = swap(back, "xh")

    limit = lax.dynamic_index_in_dim(prefix_len, (xl * 8 + z) * 2 + c, keepdims=False)
    terms = pl.pallas_call(
        attention_kernel,
        out_shape=jax.ShapeDtypeStruct((parts, rows, part), BF16),
        in_specs=[smem()] + [vmem()] * 7,
        out_specs=vmem(),
        scratch_shapes=[pltpu.VMEM((rows, w_out.shape[0]), BF16)],
        compiler_params=params(32),
        cost_estimate=pl.CostEstimate(flops=1800000000, bytes_accessed=8 << 20, transcendentals=1310720),
        name="attention",
    )(jnp.stack([xh, limit]).astype(jnp.int32), q, near, far, k, v, routed[:, part:], w_out)

    mixed = jnp.sum(spread(terms, TENSOR).astype(F32), axis=0).astype(BF16)
    here = spread(mixed.reshape(chips, slots, piece, part), CHIPS)
    there = swap(here, "c")
    home = spread(select(outward, here, there), CHIPS)
    return home.transpose(1, 0, 2, 3).reshape(slots, length, part)


def solution(mesh):
    split = Mesh(mesh.devices.reshape(2, 8, 2, 2, 4), ("xl", "z", "c", "xh", "y"))
    placed = (
        P(PROMPT, None, TENSOR),
        P(PROMPT, None, TENSOR),
        P(),
        P(None, TENSOR),
        P(None, TENSOR),
        P(None, TENSOR),
        P(TENSOR, None),
        P(PROMPT, None),
        P(),
        P(PROMPT, None),
    )
    return jax.shard_map(
        per_device,
        mesh=split,
        in_specs=placed,
        out_specs=P(PROMPT, None, TENSOR),
        check_vma=False,
    )
```

```python
import functools

import jax
import jax.numpy as jnp
from jax import lax
from jax.experimental import pallas as pl
from jax.experimental.pallas import tpu as pltpu
from jax.sharding import Mesh, PartitionSpec as P

HEAD_DIM = 128
CHIPS = ("xl", "z")
TENSOR = ("xh", "y")
PROMPT = ("xl", "z", "c")
F32 = jnp.float32
BF16 = jnp.bfloat16


def vmem():
    return pl.BlockSpec(memory_space=pltpu.VMEM)


def smem():
    return pl.BlockSpec(memory_space=pltpu.SMEM)


def anywhere():
    return pl.BlockSpec(memory_space=pltpu.HBM)


def in_hbm(x):
    return pltpu.with_memory_space_constraint(x, pltpu.HBM)


def params(mib):
    return pltpu.CompilerParams(vmem_limit_bytes=mib << 20)


def inverse_rms(total, width):
    return lax.rsqrt(total / width + 1e-05)


def dot(a, b):
    return jnp.dot(a, b, preferred_element_type=F32)


def dot_t(a, b):
    return lax.dot_general(a, b, (((1,), (1,)), ((), ())), preferred_element_type=F32)


def to_row(column, eye):
    return jnp.sum(jnp.where(eye, column, 0.0), axis=0, keepdims=True)


def to_column(row, eye):
    return jnp.sum(jnp.where(eye, row, 0.0), axis=1, keepdims=True)


def unit(size):
    return lax.broadcasted_iota(jnp.int32, (size, size), 0) == lax.broadcasted_iota(jnp.int32, (size, size), 1)


def prefix_kernel(where, gain, *refs):
    blocks, weights, (own, back, squares, x, w, acc, x_sem, w_sem) = refs[:5], refs[5:9], refs[9:]
    xh, y, c = where[0], where[1], where[2]
    parts, rows, part = x.shape
    w_copies = []
    for k, b in enumerate(weights):
        source = b.at[pl.ds(pl.multiple_of(xh * parts * part, part), parts * part), :] if k < 2 else b
        w_copies.append(pltpu.make_async_copy(source, w.at[:, pl.ds(k * HEAD_DIM, HEAD_DIM)], w_sem.at[k]))
    middle = rows // 2
    places = [x.at[0], x.at[1], x.at[2, pl.ds(0, middle), :], x.at[2, pl.ds(middle, middle), :], x.at[3]]
    x_copies = [pltpu.make_async_copy(b, p, x_sem.at[k]) for k, (b, p) in enumerate(zip(blocks, places))]
    x_copies[0].start()
    for copy in w_copies + x_copies[1:]:
        copy.start()
    total = jnp.zeros((rows, 1), F32)
    for k in range(parts):
        for copy in ([x_copies[0]], [x_copies[1]], x_copies[2:4], [x_copies[4]])[k]:
            copy.wait()
        if k == 0:
            for copy in w_copies:
                copy.wait()
        feature = (y + parts - k) & (parts - 1)
        h = x[k].astype(F32)
        total += jnp.sum(h * h, axis=1, keepdims=True)
        n = (h * gain[xh * parts + feature].astype(F32)).astype(BF16)
        term = dot(n, w[pl.ds(pl.multiple_of(feature * part, part), part), :])
        if k == 0:
            acc[...] = term
        else:
            acc[...] += term
    own[...] = acc[:, : 2 * HEAD_DIM]
    a = acc[:, 2 * HEAD_DIM : 3 * HEAD_DIM].astype(BF16)
    b = acc[:, 3 * HEAD_DIM :].astype(BF16)
    back[:, :HEAD_DIM] = jnp.where(c == 0, a, b)
    back[:, HEAD_DIM:] = jnp.where(c == 0, b, a)
    eye = unit(HEAD_DIM)
    for r in range(rows // HEAD_DIM):
        squares[r : r + 1, :] = to_row(total[r * HEAD_DIM : (r + 1) * HEAD_DIM], eye)


def state_kernel(blocks, gain, w_q, w_k, w_v, q, k, v, x, w, acc, x_sem, w_sem):
    parts, rows, part = x.shape
    split = w_q.shape[1]
    x_copies = [pltpu.make_async_copy(blocks.at[f], x.at[f], x_sem.at[f]) for f in range(parts)]
    w_copies = []
    for f in range(parts):
        at = pl.ds(f * part, part)
        w_copies.append(
            [
                pltpu.make_async_copy(w_q.at[at, :], w.at[at, pl.ds(0, split)], w_sem.at[0, f]),
                pltpu.make_async_copy(w_k.at[at, :], w.at[at, pl.ds(split, HEAD_DIM)], w_sem.at[1, f]),
                pltpu.make_async_copy(w_v.at[at, :], w.at[at, pl.ds(split + HEAD_DIM, HEAD_DIM)], w_sem.at[2, f]),
            ]
        )
    for f in range(parts):
        x_copies[f].start()
        for copy in w_copies[f]:
            copy.start()
    total = jnp.zeros((rows, 1), F32)
    for f in range(parts):
        x_copies[f].wait()
        h = x[f].astype(F32)
        total += jnp.sum(h * h, axis=1, keepdims=True)
        n = (h * gain[f].astype(F32)).astype(BF16)
        for copy in w_copies[f]:
            copy.wait()
        term = dot(n, w[f * part : (f + 1) * part, :])
        if f == 0:
            acc[...] = term
        else:
            acc[...] += term
    scale = inverse_rms(total, parts * part)
    q[...] = (acc[:, :split] * (scale * HEAD_DIM ** (-0.5))).astype(BF16)
    k[...] = (acc[:, split : split + HEAD_DIM] * scale).astype(BF16)
    v[...] = (acc[:, split + HEAD_DIM :] * scale).astype(BF16)


def attention_kernel(limit, q, own, far, squares, far_squares, k, v, meta, w_out, out, att, kv):
    rows = q.shape[0]
    length = own.shape[0]
    eye = unit(HEAD_DIM)
    for r in range(length // HEAD_DIM):
        at = slice(r * HEAD_DIM, (r + 1) * HEAD_DIM)
        total = to_column(squares[r : r + 1, :] + far_squares[r : r + 1, :], eye)
        kv[at, :] = ((own[at, :] + far[at, :].astype(F32)) * inverse_rms(total, 4096)).astype(BF16)
    near_ok = lax.broadcasted_iota(jnp.int32, (1, length), 1) < limit[0]
    pick = (lax.broadcasted_iota(jnp.int32, (8, HEAD_DIM), 1) == 1).astype(BF16)
    present = dot_t(pick, meta[...])[0:1, :] > 0.5
    a = lax.broadcasted_iota(jnp.int32, (rows, rows), 0)
    b = lax.broadcasted_iota(jnp.int32, (rows, rows), 1)
    same = ((a >> 3) & 1) == ((b >> 3) & 1)
    before = (((b >> 4) << 3) | (b & 7)) <= (((a >> 4) << 3) | (a & 7))
    own_ok = same & before & present
    for h in range(q.shape[1] // HEAD_DIM):
        at = slice(h * HEAD_DIM, (h + 1) * HEAD_DIM)
        qh = q[:, at]
        s0 = jnp.where(near_ok, dot_t(qh, kv[:, :HEAD_DIM]), -1e30)
        s1 = jnp.where(own_ok, dot_t(qh, k[...]), -1e30)
        top = jnp.maximum(jnp.max(s0, axis=1, keepdims=True), jnp.max(s1, axis=1, keepdims=True))
        p0 = jnp.where(near_ok, jnp.exp(s0 - top), 0.0)
        p1 = jnp.where(own_ok, jnp.exp(s1 - top), 0.0)
        denom = jnp.sum(p0, axis=1, keepdims=True) + jnp.sum(p1, axis=1, keepdims=True)
        numer = dot(p0.astype(BF16), kv[:, HEAD_DIM:]) + dot(p1.astype(BF16), v[...])
        att[:, at] = (numer / denom).astype(BF16)
    part = out.shape[2]

    def project(t, carry):
        at = pl.ds(pl.multiple_of(t * part, part), part)
        out[t] = dot(att[...], w_out[:, at]).astype(BF16)
        return carry

    lax.fori_loop(0, out.shape[0], project, 0)


def select_kernel(index, own, other, *rest):
    out = rest[-1]
    chips, slots = out.shape[:2]
    for q in range(chips):
        for s in range(slots):
            j = index[q, s]
            at = j & (chips - 1)
            out[q, s] = jnp.where(j < chips, own[at, s], other[at, s])


def repeat_kernel(x, *rest):
    out = rest[-1]
    for t in range(out.shape[0]):
        out[t] = x[:, : out.shape[2]]


def repeat(x, parts, part, after):
    return pl.pallas_call(
        repeat_kernel,
        out_shape=jax.ShapeDtypeStruct((parts, x.shape[0], part), x.dtype),
        in_specs=[vmem()] + [anywhere()] * len(after),
        out_specs=vmem(),
        compiler_params=params(6),
        cost_estimate=pl.CostEstimate(flops=0, bytes_accessed=2 << 20, transcendentals=0),
        name="repeat_rows",
    )(x, *after)


def select(index, own, other, after=()):
    return pl.pallas_call(
        select_kernel,
        out_shape=jax.ShapeDtypeStruct(own.shape, own.dtype),
        in_specs=[smem(), vmem(), vmem()] + [anywhere()] * len(after),
        out_specs=vmem(),
        compiler_params=params(6),
        cost_estimate=pl.CostEstimate(flops=0, bytes_accessed=3 * own.size * 2, transcendentals=0),
        name="select_blocks",
    )(index, own, other, *after)


def swap(x, axis):
    return lax.ppermute(x, axis, [(0, 1), (1, 0)])


def turn(x, s):
    return lax.ppermute(x, "y", [(i, (i + s) % 4) for i in range(4)])


def spread(x, axis):
    return lax.all_to_all(x, axis, 0, 0, tiled=True)


def blocking(lengths, x, axis):
    return lax.cond(lengths[0] > -1, lambda p: spread(p, axis), lambda p: p, x)


def per_device(
    state_hidden,
    prefix_hidden,
    norm_gain,
    w_query,
    w_key,
    w_value,
    w_out,
    scored_prompt,
    prefix_len,
    state_mask,
):
    xl, z, c = lax.axis_index("xl"), lax.axis_index("z"), lax.axis_index("c")
    xh, y = lax.axis_index("xh"), lax.axis_index("y")
    slots, length, part = state_hidden.shape
    parts = 8
    chips = 16
    piece = length // chips
    rows = slots * length
    length_p = prefix_hidden.shape[1]
    half = w_key.shape[0] // 2
    gain = norm_gain.reshape(parts, 1, part)

    prefix = prefix_hidden[0]
    left, right = turn(prefix, 1), turn(prefix, 3)
    middle = length_p // 2
    across = [turn(left[:middle], 1), turn(right[middle:], 3)]
    blocks = [prefix, left, *across, right]
    w_send = [lax.dynamic_slice_in_dim(w, (1 - xh) * half, half) for w in (w_key, w_value)]
    w_a = swap(jnp.where(c == 0, *w_send), "xh")
    w_b = swap(w_a, "c")

    lane = lax.broadcasted_iota(jnp.int32, (slots, length, HEAD_DIM), 2)
    meta = jnp.where(lane == 0, scored_prompt[0][:, None, None], state_mask[:, :, None])
    meta = jnp.where(lane < 2, meta, 0).astype(BF16)
    packed = jnp.concatenate([state_hidden, meta], axis=2)
    packed = packed.reshape(slots, chips, piece, part + HEAD_DIM).transpose(1, 0, 2, 3)
    here = spread(packed, CHIPS)
    there = swap(here, "c")
    ids = here[:, :, 0, part].astype(jnp.int32)
    ids_there = there[:, :, 0, part].astype(jnp.int32)
    chip = jnp.arange(chips, dtype=jnp.int32)
    wanted = (2 * chip + c)[:, None, None]
    inward = jnp.sum(
        jnp.where(ids[None] == wanted, chip[None, :, None], 0)
        + jnp.where(ids_there[None] == wanted, chips + chip[None, :, None], 0),
        axis=1,
    ).astype(jnp.int32)
    outward = jnp.where(ids % 2 == c, ids // 2, chips + ids // 2)
    routed = spread(select(inward, here, there, [w_a]), CHIPS).reshape(rows, part + HEAD_DIM)

    wide = repeat(routed, parts, part, across)
    wide = spread(wide, TENSOR)
    place = jnp.stack([xh, y, c]).astype(jnp.int32)
    own, back, squares = pl.pallas_call(
        prefix_kernel,
        out_shape=[
            jax.ShapeDtypeStruct((length_p, 2 * HEAD_DIM), F32),
            jax.ShapeDtypeStruct((length_p, 2 * HEAD_DIM), BF16),
            jax.ShapeDtypeStruct((length_p // HEAD_DIM, HEAD_DIM), F32),
        ],
        in_specs=[smem(), vmem()] + [anywhere()] * 9,
        out_specs=[vmem()] * 3,
        scratch_shapes=[
            pltpu.VMEM((4, length_p, part), BF16),
            pltpu.VMEM((half, 4 * HEAD_DIM), BF16),
            pltpu.VMEM((length_p, 4 * HEAD_DIM), F32),
            pltpu.SemaphoreType.DMA((5,)),
            pltpu.SemaphoreType.DMA((4,)),
        ],
        compiler_params=params(18),
        cost_estimate=pl.CostEstimate(flops=2147483648, bytes_accessed=8 << 20, transcendentals=0),
        name="prefix_projection",
    )(place, gain, *blocks, in_hbm(w_key), in_hbm(w_value), w_a, w_b)
    far, far_squares = swap(back, "xh"), swap(squares, "xh")

    q, k, v = pl.pallas_call(
        state_kernel,
        out_shape=[
            jax.ShapeDtypeStruct((rows, w_query.shape[1]), BF16),
            jax.ShapeDtypeStruct((rows, HEAD_DIM), BF16),
            jax.ShapeDtypeStruct((rows, HEAD_DIM), BF16),
        ],
        in_specs=[anywhere(), vmem()] + [anywhere()] * 3,
        out_specs=[vmem()] * 3,
        scratch_shapes=[
            pltpu.VMEM((parts, rows, part), BF16),
            pltpu.VMEM((parts * part, w_query.shape[1] + 2 * HEAD_DIM), BF16),
            pltpu.VMEM((rows, w_query.shape[1] + 2 * HEAD_DIM), F32),
            pltpu.SemaphoreType.DMA((parts,)),
            pltpu.SemaphoreType.DMA((3, parts)),
        ],
        compiler_params=params(14),
        cost_estimate=pl.CostEstimate(flops=1610612736, bytes_accessed=8 << 20, transcendentals=0),
        name="state_projection",
    )(in_hbm(wide), gain, in_hbm(w_query), in_hbm(w_key), in_hbm(w_value))

    limit = lax.dynamic_index_in_dim(prefix_len, (xl * 8 + z) * 2 + c, keepdims=False)
    terms = pl.pallas_call(
        attention_kernel,
        out_shape=jax.ShapeDtypeStruct((parts, rows, part), BF16),
        in_specs=[smem()] + [vmem()] * 9,
        out_specs=vmem(),
        scratch_shapes=[
            pltpu.VMEM((rows, w_out.shape[0]), BF16),
            pltpu.VMEM((length_p, 2 * HEAD_DIM), BF16),
        ],
        compiler_params=params(20),
        cost_estimate=pl.CostEstimate(flops=1800000000, bytes_accessed=8 << 20, transcendentals=1310720),
        name="attention",
    )(limit[None], q, own, far, squares, far_squares, k, v, routed[:, part:], w_out)

    mixed = jnp.sum(spread(terms, TENSOR).astype(F32), axis=0).astype(BF16)
    here = spread(mixed.reshape(chips, slots, piece, part), CHIPS)
    there = swap(here, "c")
    home = spread(select(outward, here, there), CHIPS)
    return home.transpose(1, 0, 2, 3).reshape(slots, length, part)


def solution(mesh):
    split = Mesh(mesh.devices.reshape(2, 8, 2, 2, 4), ("xl", "z", "c", "xh", "y"))
    placed = (
        P(PROMPT, None, TENSOR),
        P(PROMPT, None, TENSOR),
        P(),
        P(None, TENSOR),
        P(None, TENSOR),
        P(None, TENSOR),
        P(TENSOR, None),
        P(PROMPT, None),
        P(),
        P(PROMPT, None),
    )
    return jax.shard_map(
        per_device,
        mesh=split,
        in_specs=placed,
        out_specs=P(PROMPT, None, TENSOR),
        check_vma=False,
    )
```

```python
import functools

import jax
import jax.numpy as jnp
from jax import lax
from jax.experimental import pallas as pl
from jax.experimental.pallas import tpu as pltpu
from jax.sharding import Mesh, PartitionSpec as P

HEAD_DIM = 128
CHIPS = ("xl", "z")
TENSOR = ("xh", "y")
PROMPT = ("xl", "z", "c")
F32 = jnp.float32
BF16 = jnp.bfloat16


def vmem():
    return pl.BlockSpec(memory_space=pltpu.VMEM)


def smem():
    return pl.BlockSpec(memory_space=pltpu.SMEM)


def anywhere():
    return pl.BlockSpec(memory_space=pltpu.HBM)


def in_hbm(x):
    return pltpu.with_memory_space_constraint(x, pltpu.HBM)


def params(mib):
    return pltpu.CompilerParams(vmem_limit_bytes=mib << 20)


def inverse_rms(total, width):
    return lax.rsqrt(total / width + 1e-05)


def dot(a, b):
    return jnp.dot(a, b, preferred_element_type=F32)


def dot_t(a, b):
    return lax.dot_general(a, b, (((1,), (1,)), ((), ())), preferred_element_type=F32)


def to_row(column, eye):
    return jnp.sum(jnp.where(eye, column, 0.0), axis=0, keepdims=True)


def to_column(row, eye):
    return jnp.sum(jnp.where(eye, row, 0.0), axis=1, keepdims=True)


def unit(size):
    return lax.broadcasted_iota(jnp.int32, (size, size), 0) == lax.broadcasted_iota(jnp.int32, (size, size), 1)


def prefix_kernel(where, gain, *refs):
    blocks, weights, (own, back, squares, x, w, acc, x_sem, w_sem) = refs[:7], refs[7:11], refs[11:]
    xh, y, c = where[0], where[1], where[2]
    parts, rows, part = x.shape
    w_copies = []
    for k, b in enumerate(weights):
        source = b.at[pl.ds(pl.multiple_of(xh * parts * part, part), parts * part), :] if k < 2 else b
        w_copies.append(pltpu.make_async_copy(source, w.at[:, pl.ds(k * HEAD_DIM, HEAD_DIM)], w_sem.at[k]))
    middle = rows // 2
    places = [x.at[0]] + [x.at[k, pl.ds(r * middle, middle), :] for k in (1, 2, 3) for r in (0, 1)]
    x_copies = [pltpu.make_async_copy(b, p, x_sem.at[k]) for k, (b, p) in enumerate(zip(blocks, places))]
    x_copies[0].start()
    for copy in w_copies + x_copies[1:]:
        copy.start()
    total = jnp.zeros((rows, 1), F32)
    for k in range(parts):
        for copy in x_copies[:1] if k == 0 else x_copies[2 * k - 1 : 2 * k + 1]:
            copy.wait()
        if k == 0:
            for copy in w_copies:
                copy.wait()
        feature = (y + parts - k) & (parts - 1)
        h = x[k].astype(F32)
        total += jnp.sum(h * h, axis=1, keepdims=True)
        n = (h * gain[xh * parts + feature].astype(F32)).astype(BF16)
        term = dot(n, w[pl.ds(pl.multiple_of(feature * part, part), part), :])
        if k == 0:
            acc[...] = term
        else:
            acc[...] += term
    own[...] = acc[:, : 2 * HEAD_DIM]
    a = acc[:, 2 * HEAD_DIM : 3 * HEAD_DIM].astype(BF16)
    b = acc[:, 3 * HEAD_DIM :].astype(BF16)
    back[:, :HEAD_DIM] = jnp.where(c == 0, a, b)
    back[:, HEAD_DIM:] = jnp.where(c == 0, b, a)
    eye = unit(HEAD_DIM)
    for r in range(rows // HEAD_DIM):
        squares[r : r + 1, :] = to_row(total[r * HEAD_DIM : (r + 1) * HEAD_DIM], eye)


def state_kernel(x, gain, w_q, w_k, w_v, q, k, v, w, sem):
    parts, rows, part = x.shape
    split = w_q.shape[1]
    half = parts * part // 2
    copies = []
    for r in range(2):
        at = pl.ds(r * half, half)
        places = (pl.ds(0, split), pl.ds(split, HEAD_DIM), pl.ds(split + HEAD_DIM, HEAD_DIM))
        copies.append(
            [
                pltpu.make_async_copy(b.at[at, :], w.at[at, p], sem.at[r, j])
                for j, (b, p) in enumerate(zip((w_q, w_k, w_v), places))
            ]
        )
    for copy in copies[0] + copies[1]:
        copy.start()
    squares = jnp.zeros((rows, part), F32)
    normed = []
    for f in range(parts):
        h = x[f].astype(F32)
        squares += h * h
        normed.append((h * gain[f].astype(F32)).astype(BF16))
    scale = inverse_rms(jnp.sum(squares, axis=1, keepdims=True), parts * part)
    total = None
    for r in range(2):
        for copy in copies[r]:
            copy.wait()
        n = jnp.concatenate(normed[r * parts // 2 : (r + 1) * parts // 2], axis=1)
        term = dot(n, w[r * half : (r + 1) * half, :])
        total = term if r == 0 else total + term
    q[...] = (total[:, :split] * (scale * HEAD_DIM ** (-0.5))).astype(BF16)
    k[...] = (total[:, split : split + HEAD_DIM] * scale).astype(BF16)
    v[...] = (total[:, split + HEAD_DIM :] * scale).astype(BF16)


def attention_kernel(limit, q, own, far, squares, far_squares, k, v, meta, w_out, out, att, kv):
    rows = q.shape[0]
    length = own.shape[0]
    eye = unit(HEAD_DIM)
    for r in range(length // HEAD_DIM):
        at = slice(r * HEAD_DIM, (r + 1) * HEAD_DIM)
        total = to_column(squares[r : r + 1, :] + far_squares[r : r + 1, :], eye)
        kv[at, :] = ((own[at, :] + far[at, :].astype(F32)) * inverse_rms(total, 4096)).astype(BF16)
    kv[length:, :HEAD_DIM] = k[...]
    kv[length:, HEAD_DIM:] = v[...]
    near = jnp.where(lax.broadcasted_iota(jnp.int32, (1, length), 1) < limit[0], 0.0, -1e30)
    pick = (lax.broadcasted_iota(jnp.int32, (8, HEAD_DIM), 1) == 1).astype(BF16)
    present = dot_t(pick, meta[...])[0:1, :] > 0.5
    a = lax.broadcasted_iota(jnp.int32, (rows, rows), 0)
    b = lax.broadcasted_iota(jnp.int32, (rows, rows), 1)
    same = ((a >> 3) & 1) == ((b >> 3) & 1)
    before = (((b >> 4) << 3) | (b & 7)) <= (((a >> 4) << 3) | (a & 7))
    own_ok = same & before & present
    for h in range(q.shape[1] // HEAD_DIM):
        at = slice(h * HEAD_DIM, (h + 1) * HEAD_DIM)
        s = dot_t(q[:, at], kv[:, :HEAD_DIM])
        s0 = s[:, :length] + near
        s1 = jnp.where(own_ok, s[:, length:], -1e30)
        top = jnp.maximum(jnp.max(s0, axis=1, keepdims=True), jnp.max(s1, axis=1, keepdims=True))
        p0 = jnp.exp(s0 - top)
        p1 = jnp.exp(s1 - top)
        denom = jnp.sum(p0, axis=1, keepdims=True) + jnp.sum(p1, axis=1, keepdims=True)
        p = jnp.concatenate([p0.astype(BF16), p1.astype(BF16)], axis=1)
        numer = dot(p, kv[:, HEAD_DIM:])
        att[:, at] = (numer / denom).astype(BF16)
    part = out.shape[2]
    for t in range(out.shape[0]):
        out[t] = dot(att[...], w_out[:, t * part : (t + 1) * part]).astype(BF16)


def pack_kernel(where, ids, hidden, mask, prefix, w_k, w_v, out, top, bottom, w_half, sem):
    slots, length, part = hidden.shape
    pieces = length // 8
    middle = prefix.shape[0] // 2
    half = w_half.shape[0]
    rows = pl.ds(pl.multiple_of((1 - where[0]) * half, half), half)
    halves = [
        pltpu.make_async_copy(prefix.at[pl.ds(0, middle), :], top, sem.at[0]),
        pltpu.make_async_copy(prefix.at[pl.ds(middle, middle), :], bottom, sem.at[1]),
    ]
    key = pltpu.make_async_copy(w_k.at[rows, :], w_half, sem.at[2])
    value = pltpu.make_async_copy(w_v.at[rows, :], w_half, sem.at[2])
    for copy in halves:
        copy.start()
    pl.when(where[2] == 0)(key.start)
    pl.when(where[2] != 0)(value.start)
    eye = unit(length)
    lane = lax.broadcasted_iota(jnp.int32, (length, HEAD_DIM), 1)
    for s in range(slots):
        present = to_column(mask[s : s + 1, :].astype(F32), eye)
        meta = jnp.where(lane == 0, ids[0, s].astype(F32), jnp.where(lane == 1, present, 0.0))
        out[:, s, :, :part] = hidden[s].astype(F32).reshape(pieces, 8, part).astype(BF16)
        out[:, s, :, part:] = meta.reshape(pieces, 8, HEAD_DIM).astype(BF16)
    for copy in halves:
        copy.wait()
    key.wait()


def select_kernel(index, own, other, *rest):
    out = rest[-1]
    chips, slots = out.shape[:2]
    for q in range(chips):
        for s in range(slots):
            j = index[q, s]
            at = j & (chips - 1)
            out[q, s] = jnp.where(j < chips, own[at, s], other[at, s])


def repeat_kernel(x, *rest):
    out = rest[-1]
    for t in range(out.shape[0]):
        out[t] = x[:, : out.shape[2]]


def repeat(x, parts, part, after):
    return pl.pallas_call(
        repeat_kernel,
        out_shape=jax.ShapeDtypeStruct((parts, x.shape[0], part), x.dtype),
        in_specs=[vmem()] + [anywhere()] * len(after),
        out_specs=vmem(),
        compiler_params=params(6),
        cost_estimate=pl.CostEstimate(flops=0, bytes_accessed=2 << 20, transcendentals=0),
        name="repeat_rows",
    )(x, *after)


def mark_kernel(*refs):
    refs[-1][...] = jnp.zeros(refs[-1].shape, F32)


def mark(after, flops):
    return pl.pallas_call(
        mark_kernel,
        out_shape=jax.ShapeDtypeStruct((8, HEAD_DIM), F32),
        in_specs=[anywhere()] * len(after),
        out_specs=vmem(),
        compiler_params=params(2),
        cost_estimate=pl.CostEstimate(flops=flops, bytes_accessed=4096, transcendentals=0),
        name="arrived",
    )(*after)


def select(index, own, other, after=()):
    return pl.pallas_call(
        select_kernel,
        out_shape=jax.ShapeDtypeStruct(own.shape, own.dtype),
        in_specs=[smem(), vmem(), vmem()] + [anywhere()] * len(after),
        out_specs=vmem(),
        compiler_params=params(6),
        cost_estimate=pl.CostEstimate(flops=0, bytes_accessed=3 * own.size * 2, transcendentals=0),
        name="select_blocks",
    )(index, own, other, *after)


def swap(x, axis):
    return lax.ppermute(x, axis, [(0, 1), (1, 0)])


def turn(x, s):
    return lax.ppermute(x, "y", [(i, (i + s) % 4) for i in range(4)])


def spread(x, axis):
    return lax.all_to_all(x, axis, 0, 0, tiled=True)


def blocking(lengths, x, axis):
    return lax.cond(lengths[0] > -1, lambda p: spread(p, axis), lambda p: p, x)


def per_device(
    state_hidden,
    prefix_hidden,
    norm_gain,
    w_query,
    w_key,
    w_value,
    w_out,
    scored_prompt,
    prefix_len,
    state_mask,
):
    xl, z, c = lax.axis_index("xl"), lax.axis_index("z"), lax.axis_index("c")
    xh, y = lax.axis_index("xh"), lax.axis_index("y")
    slots, length, part = state_hidden.shape
    parts = 8
    chips = 16
    piece = length // chips
    rows = slots * length
    length_p = prefix_hidden.shape[1]
    half = w_key.shape[0] // 2
    gain = norm_gain.reshape(parts, 1, part)

    place = jnp.stack([xh, y, c]).astype(jnp.int32)
    prefix = prefix_hidden[0]
    middle = length_p // 2
    packed, top, bottom, w_send = pl.pallas_call(
        pack_kernel,
        out_shape=[
            jax.ShapeDtypeStruct((chips, slots, piece, part + HEAD_DIM), BF16),
            jax.ShapeDtypeStruct((middle, part), BF16),
            jax.ShapeDtypeStruct((middle, part), BF16),
            jax.ShapeDtypeStruct((half, HEAD_DIM), BF16),
        ],
        in_specs=[smem(), smem(), vmem(), vmem()] + [anywhere()] * 3,
        out_specs=[vmem()] * 4,
        scratch_shapes=[pltpu.SemaphoreType.DMA((3,))],
        compiler_params=params(10),
        cost_estimate=pl.CostEstimate(flops=0, bytes_accessed=4 << 20, transcendentals=0),
        name="pack_states",
    )(place, in_hbm(scored_prompt), *[in_hbm(x) for x in (state_hidden, state_mask, prefix, w_key, w_value)])

    first = [turn(top, 1), turn(bottom, 3)]
    second = [turn(bottom, 1), turn(top, 3), turn(first[0], 1), turn(first[1], 3)]
    blocks = [prefix, first[0], second[0], second[2], second[3], second[1], first[1]]
    w_a = swap(w_send, "xh")
    w_b = swap(w_a, "c")

    here = spread(packed, CHIPS)
    there = swap(here, "c")
    ids = here[:, :, 0, part].astype(jnp.int32)
    ids_there = there[:, :, 0, part].astype(jnp.int32)
    chip = jnp.arange(chips, dtype=jnp.int32)
    wanted = (2 * chip + c)[:, None, None]
    inward = jnp.sum(
        jnp.where(ids[None] == wanted, chip[None, :, None], 0)
        + jnp.where(ids_there[None] == wanted, chips + chip[None, :, None], 0),
        axis=1,
    ).astype(jnp.int32)
    outward = jnp.where(ids % 2 == c, ids // 2, chips + ids // 2)
    routed = spread(select(inward, here, there, [mark(first, 10**9)]), CHIPS).reshape(rows, part + HEAD_DIM)

    wide = repeat(routed, parts, part, [mark(second, 10**9), w_b])
    wide = spread(wide, TENSOR)
    own, back, squares = pl.pallas_call(
        prefix_kernel,
        out_shape=[
            jax.ShapeDtypeStruct((length_p, 2 * HEAD_DIM), F32),
            jax.ShapeDtypeStruct((length_p, 2 * HEAD_DIM), BF16),
            jax.ShapeDtypeStruct((length_p // HEAD_DIM, HEAD_DIM), F32),
        ],
        in_specs=[smem(), vmem()] + [anywhere()] * 11,
        out_specs=[vmem()] * 3,
        scratch_shapes=[
            pltpu.VMEM((4, length_p, part), BF16),
            pltpu.VMEM((half, 4 * HEAD_DIM), BF16),
            pltpu.VMEM((length_p, 4 * HEAD_DIM), F32),
            pltpu.SemaphoreType.DMA((7,)),
            pltpu.SemaphoreType.DMA((4,)),
        ],
        compiler_params=params(18),
        cost_estimate=pl.CostEstimate(flops=2147483648, bytes_accessed=8 << 20, transcendentals=0),
        name="prefix_projection",
    )(place, gain, *[in_hbm(x) for x in [*blocks, w_key, w_value, w_a, w_b]])
    far, far_squares = swap(back, "xh"), swap(squares, "xh")

    q, k, v = pl.pallas_call(
        state_kernel,
        out_shape=[
            jax.ShapeDtypeStruct((rows, w_query.shape[1]), BF16),
            jax.ShapeDtypeStruct((rows, HEAD_DIM), BF16),
            jax.ShapeDtypeStruct((rows, HEAD_DIM), BF16),
        ],
        in_specs=[vmem()] * 2 + [anywhere()] * 3,
        out_specs=[vmem()] * 3,
        scratch_shapes=[
            pltpu.VMEM((parts * part, w_query.shape[1] + 2 * HEAD_DIM), BF16),
            pltpu.SemaphoreType.DMA((2, 3)),
        ],
        compiler_params=params(20),
        cost_estimate=pl.CostEstimate(flops=1610612736, bytes_accessed=8 << 20, transcendentals=0),
        name="state_projection",
    )(wide, gain, in_hbm(w_query), in_hbm(w_key), in_hbm(w_value))

    limit = lax.dynamic_index_in_dim(prefix_len, (xl * 8 + z) * 2 + c, keepdims=False)
    terms = pl.pallas_call(
        attention_kernel,
        out_shape=jax.ShapeDtypeStruct((parts, rows, part), BF16),
        in_specs=[smem()] + [vmem()] * 9,
        out_specs=vmem(),
        scratch_shapes=[
            pltpu.VMEM((rows, w_out.shape[0]), BF16),
            pltpu.VMEM((length_p + rows, 2 * HEAD_DIM), BF16),
        ],
        compiler_params=params(24),
        cost_estimate=pl.CostEstimate(flops=1800000000, bytes_accessed=8 << 20, transcendentals=1310720),
        name="attention",
    )(limit[None], q, own, far, squares, far_squares, k, v, routed[:, part:], w_out)

    mixed = jnp.sum(spread(terms, TENSOR).astype(F32), axis=0).astype(BF16)
    here = spread(mixed.reshape(chips, slots, piece, part), CHIPS)
    there = swap(here, "c")
    home = spread(select(outward, here, there), CHIPS)
    return home.transpose(1, 0, 2, 3).reshape(slots, length, part)


def solution(mesh):
    split = Mesh(mesh.devices.reshape(2, 8, 2, 2, 4), ("xl", "z", "c", "xh", "y"))
    placed = (
        P(PROMPT, None, TENSOR),
        P(PROMPT, None, TENSOR),
        P(),
        P(None, TENSOR),
        P(None, TENSOR),
        P(None, TENSOR),
        P(TENSOR, None),
        P(PROMPT, None),
        P(),
        P(PROMPT, None),
    )
    return jax.shard_map(
        per_device,
        mesh=split,
        in_specs=placed,
        out_specs=P(PROMPT, None, TENSOR),
        check_vma=False,
    )
```

```python
import functools

import jax
import jax.numpy as jnp
from jax import lax
from jax.experimental import pallas as pl
from jax.experimental.pallas import tpu as pltpu
from jax.sharding import Mesh, PartitionSpec as P

HEAD_DIM = 128
CHIPS = ("xl", "z")
TENSOR = ("xh", "y")
PROMPT = ("xl", "z", "c")
F32 = jnp.float32
BF16 = jnp.bfloat16


def vmem():
    return pl.BlockSpec(memory_space=pltpu.VMEM)


def smem():
    return pl.BlockSpec(memory_space=pltpu.SMEM)


def anywhere():
    return pl.BlockSpec(memory_space=pltpu.HBM)


def in_hbm(x):
    return pltpu.with_memory_space_constraint(x, pltpu.HBM)


def in_vmem(x):
    return pltpu.with_memory_space_constraint(x, pltpu.VMEM)


def params(mib):
    return pltpu.CompilerParams(vmem_limit_bytes=mib << 20)


def inverse_rms(total, width):
    return lax.rsqrt(total / width + 1e-05)


def dot(a, b):
    return jnp.dot(a, b, preferred_element_type=F32)


def dot_t(a, b):
    return lax.dot_general(a, b, (((1,), (1,)), ((), ())), preferred_element_type=F32)


def to_row(column, eye):
    return jnp.sum(jnp.where(eye, column, 0.0), axis=0, keepdims=True)


def to_column(row, eye):
    return jnp.sum(jnp.where(eye, row, 0.0), axis=1, keepdims=True)


def unit(size):
    return lax.broadcasted_iota(jnp.int32, (size, size), 0) == lax.broadcasted_iota(jnp.int32, (size, size), 1)


def prefix_kernel(where, gain, *refs):
    blocks, weights, (own, back, squares, x, w, acc, x_sem, w_sem) = refs[:7], refs[7:10], refs[10:]
    xh, y = where[0], where[1]
    parts, rows, part = x.shape
    w_copies = []
    for k, b in enumerate(weights):
        source = b.at[pl.ds(pl.multiple_of(xh * parts * part, part), parts * part), :] if k < 2 else b
        place = w.at[:, pl.ds(k * HEAD_DIM, b.shape[1])]
        w_copies.append(pltpu.make_async_copy(source, place, w_sem.at[k]))
    middle = rows // 2
    places = [x.at[0]] + [x.at[k, pl.ds(r * middle, middle), :] for k in (1, 2, 3) for r in (0, 1)]
    x_copies = [pltpu.make_async_copy(b, p, x_sem.at[k]) for k, (b, p) in enumerate(zip(blocks, places))]
    x_copies[0].start()
    for copy in w_copies + x_copies[1:]:
        copy.start()
    total = jnp.zeros((rows, 1), F32)
    for k in range(parts):
        for copy in x_copies[:1] if k == 0 else x_copies[2 * k - 1 : 2 * k + 1]:
            copy.wait()
        if k == 0:
            for copy in w_copies:
                copy.wait()
        feature = (y + parts - k) & (parts - 1)
        h = x[k].astype(F32)
        total += jnp.sum(h * h, axis=1, keepdims=True)
        n = (h * gain[xh * parts + feature].astype(F32)).astype(BF16)
        term = dot(n, w[pl.ds(pl.multiple_of(feature * part, part), part), :])
        if k == 0:
            acc[...] = term
        else:
            acc[...] += term
    own[...] = acc[:, : 2 * HEAD_DIM]
    back[...] = acc[:, 2 * HEAD_DIM :].astype(BF16)
    eye = unit(HEAD_DIM)
    for r in range(rows // HEAD_DIM):
        squares[r : r + 1, :] = to_row(total[r * HEAD_DIM : (r + 1) * HEAD_DIM], eye)


def state_kernel(x, gain, w_q, w_k, w_v, q, k, v, w, sem):
    parts, rows, part = x.shape
    split = w_q.shape[1]
    half = parts * part // 2
    copies = []
    for r in range(2):
        at = pl.ds(r * half, half)
        places = (pl.ds(0, split), pl.ds(split, HEAD_DIM), pl.ds(split + HEAD_DIM, HEAD_DIM))
        copies.append(
            [
                pltpu.make_async_copy(b.at[at, :], w.at[at, p], sem.at[r, j])
                for j, (b, p) in enumerate(zip((w_q, w_k, w_v), places))
            ]
        )
    for copy in copies[0] + copies[1]:
        copy.start()
    squares = jnp.zeros((rows, part), F32)
    normed = []
    for f in range(parts):
        h = x[f].astype(F32)
        squares += h * h
        normed.append((h * gain[f].astype(F32)).astype(BF16))
    scale = inverse_rms(jnp.sum(squares, axis=1, keepdims=True), parts * part)
    total = None
    for r in range(2):
        for copy in copies[r]:
            copy.wait()
        n = jnp.concatenate(normed[r * parts // 2 : (r + 1) * parts // 2], axis=1)
        term = dot(n, w[r * half : (r + 1) * half, :])
        total = term if r == 0 else total + term
    q[...] = (total[:, :split] * (scale * HEAD_DIM ** (-0.5))).astype(BF16)
    k[...] = (total[:, split : split + HEAD_DIM] * scale).astype(BF16)
    v[...] = (total[:, split + HEAD_DIM :] * scale).astype(BF16)


def attention_kernel(limit, q, own, far, squares, far_squares, k, v, meta, w_out, out, att, kv):
    rows = q.shape[0]
    length = own.shape[0]
    eye = unit(HEAD_DIM)
    for r in range(length // HEAD_DIM):
        at = slice(r * HEAD_DIM, (r + 1) * HEAD_DIM)
        total = to_column(squares[r : r + 1, :] + far_squares[r : r + 1, :], eye)
        kv[at, :] = ((own[at, :] + far[at, :].astype(F32)) * inverse_rms(total, 4096)).astype(BF16)
    kv[length:, :HEAD_DIM] = k[...]
    kv[length:, HEAD_DIM:] = v[...]
    near = jnp.where(lax.broadcasted_iota(jnp.int32, (1, length), 1) < limit[0], 0.0, -1e30)
    pick = (lax.broadcasted_iota(jnp.int32, (8, HEAD_DIM), 1) == 1).astype(BF16)
    present = dot_t(pick, meta[...])[0:1, :] > 0.5
    a = lax.broadcasted_iota(jnp.int32, (rows, rows), 0)
    b = lax.broadcasted_iota(jnp.int32, (rows, rows), 1)
    same = ((a >> 3) & 1) == ((b >> 3) & 1)
    before = (((b >> 4) << 3) | (b & 7)) <= (((a >> 4) << 3) | (a & 7))
    own_ok = same & before & present
    for h in range(q.shape[1] // HEAD_DIM):
        at = slice(h * HEAD_DIM, (h + 1) * HEAD_DIM)
        s = dot_t(q[:, at], kv[:, :HEAD_DIM])
        s0 = s[:, :length] + near
        s1 = jnp.where(own_ok, s[:, length:], -1e30)
        top = jnp.maximum(jnp.max(s0, axis=1, keepdims=True), jnp.max(s1, axis=1, keepdims=True))
        p0 = jnp.exp(s0 - top)
        p1 = jnp.exp(s1 - top)
        denom = jnp.sum(p0, axis=1, keepdims=True) + jnp.sum(p1, axis=1, keepdims=True)
        p = jnp.concatenate([p0.astype(BF16), p1.astype(BF16)], axis=1)
        numer = dot(p, kv[:, HEAD_DIM:])
        att[:, at] = (numer / denom).astype(BF16)
    part = out.shape[2]
    for t in range(out.shape[0]):
        out[t] = dot(att[...], w_out[:, t * part : (t + 1) * part]).astype(BF16)


def pack_kernel(where, ids, hidden, mask, prefix, w_k, w_v, out, top, bottom, w_half, sem):
    slots, length, part = hidden.shape
    pieces = length // 8
    middle = prefix.shape[0] // 2
    half = w_half.shape[0]
    rows = pl.ds(pl.multiple_of((1 - where[0]) * half, half), half)
    halves = [
        pltpu.make_async_copy(prefix.at[pl.ds(0, middle), :], top, sem.at[0]),
        pltpu.make_async_copy(prefix.at[pl.ds(middle, middle), :], bottom, sem.at[1]),
    ]
    halves.append(pltpu.make_async_copy(w_k.at[rows, :], w_half.at[:, pl.ds(0, HEAD_DIM)], sem.at[2]))
    halves.append(pltpu.make_async_copy(w_v.at[rows, :], w_half.at[:, pl.ds(HEAD_DIM, HEAD_DIM)], sem.at[3]))
    for copy in halves:
        copy.start()
    eye = unit(length)
    lane = lax.broadcasted_iota(jnp.int32, (length, HEAD_DIM), 1)
    for s in range(slots):
        present = to_column(mask[s : s + 1, :].astype(F32), eye)
        meta = jnp.where(lane == 0, ids[0, s].astype(F32), jnp.where(lane == 1, present, 0.0))
        out[:, s, :, :part] = hidden[s].astype(F32).reshape(pieces, 8, part).astype(BF16)
        out[:, s, :, part:] = meta.reshape(pieces, 8, HEAD_DIM).astype(BF16)
    for copy in halves:
        copy.wait()


def select_kernel(index, own, other, *rest):
    out = rest[-1]
    chips, slots = out.shape[:2]
    for q in range(chips):
        for s in range(slots):
            j = index[q, s]
            at = j & (chips - 1)
            out[q, s] = jnp.where(j < chips, own[at, s], other[at, s])


def repeat_kernel(x, *rest):
    out = rest[-1]
    for t in range(out.shape[0]):
        out[t] = x[:, : out.shape[2]]


def repeat(x, parts, part, after):
    return pl.pallas_call(
        repeat_kernel,
        out_shape=jax.ShapeDtypeStruct((parts, x.shape[0], part), x.dtype),
        in_specs=[vmem()] + [anywhere()] * len(after),
        out_specs=vmem(),
        compiler_params=params(6),
        cost_estimate=pl.CostEstimate(flops=0, bytes_accessed=2 << 20, transcendentals=0),
        name="repeat_rows",
    )(x, *after)


def mark_kernel(*refs):
    refs[-1][...] = jnp.zeros(refs[-1].shape, F32)


def mark(after, flops):
    return pl.pallas_call(
        mark_kernel,
        out_shape=jax.ShapeDtypeStruct((8, HEAD_DIM), F32),
        in_specs=[anywhere()] * len(after),
        out_specs=vmem(),
        compiler_params=params(2),
        cost_estimate=pl.CostEstimate(flops=flops, bytes_accessed=4096, transcendentals=0),
        name="arrived",
    )(*after)


def select(index, own, other, after=()):
    return pl.pallas_call(
        select_kernel,
        out_shape=jax.ShapeDtypeStruct(own.shape, own.dtype),
        in_specs=[smem(), vmem(), vmem()] + [anywhere()] * len(after),
        out_specs=vmem(),
        compiler_params=params(6),
        cost_estimate=pl.CostEstimate(flops=0, bytes_accessed=3 * own.size * 2, transcendentals=0),
        name="select_blocks",
    )(index, own, other, *after)


def swap(x, axis):
    return lax.ppermute(x, axis, [(0, 1), (1, 0)])


def turn(x, s):
    return lax.ppermute(x, "y", [(i, (i + s) % 4) for i in range(4)])


def spread(x, axis):
    return lax.all_to_all(x, axis, 0, 0, tiled=True)


def blocking(lengths, x, axis):
    return lax.cond(lengths[0] > -1, lambda p: spread(p, axis), lambda p: p, x)


def per_device(
    state_hidden,
    prefix_hidden,
    norm_gain,
    w_query,
    w_key,
    w_value,
    w_out,
    scored_prompt,
    prefix_len,
    state_mask,
):
    xl, z, c = lax.axis_index("xl"), lax.axis_index("z"), lax.axis_index("c")
    xh, y = lax.axis_index("xh"), lax.axis_index("y")
    slots, length, part = state_hidden.shape
    parts = 8
    chips = 16
    piece = length // chips
    rows = slots * length
    length_p = prefix_hidden.shape[1]
    half = w_key.shape[0] // 2
    gain = norm_gain.reshape(parts, 1, part)

    place = jnp.stack([xh, y, c]).astype(jnp.int32)
    prefix = prefix_hidden[0]
    middle = length_p // 2
    packed, top, bottom, w_send = pl.pallas_call(
        pack_kernel,
        out_shape=[
            jax.ShapeDtypeStruct((chips, slots, piece, part + HEAD_DIM), BF16),
            jax.ShapeDtypeStruct((middle, part), BF16),
            jax.ShapeDtypeStruct((middle, part), BF16),
            jax.ShapeDtypeStruct((half, 2 * HEAD_DIM), BF16),
        ],
        in_specs=[smem(), smem(), vmem(), vmem()] + [anywhere()] * 3,
        out_specs=[vmem()] * 4,
        scratch_shapes=[pltpu.SemaphoreType.DMA((4,))],
        compiler_params=params(12),
        cost_estimate=pl.CostEstimate(flops=0, bytes_accessed=4 << 20, transcendentals=0),
        name="pack_states",
    )(place, in_hbm(scored_prompt), *[in_hbm(x) for x in (state_hidden, state_mask, prefix, w_key, w_value)])

    first = [turn(top, 1), turn(bottom, 3)]
    second = [turn(bottom, 1), turn(top, 3), turn(first[0], 1), turn(first[1], 3)]
    blocks = [prefix, first[0], second[0], second[2], second[3], second[1], first[1]]
    w_a = swap(w_send, "xh")

    here = spread(packed, CHIPS)
    there = swap(here, "c")
    ids = here[:, :, 0, part].astype(jnp.int32)
    ids_there = there[:, :, 0, part].astype(jnp.int32)
    chip = jnp.arange(chips, dtype=jnp.int32)
    wanted = (2 * chip + c)[:, None, None]
    inward = jnp.sum(
        jnp.where(ids[None] == wanted, chip[None, :, None], 0)
        + jnp.where(ids_there[None] == wanted, chips + chip[None, :, None], 0),
        axis=1,
    ).astype(jnp.int32)
    outward = jnp.where(ids % 2 == c, ids // 2, chips + ids // 2)
    routed = spread(select(inward, here, there, [mark(first, 10**9)]), CHIPS).reshape(rows, part + HEAD_DIM)

    wide = repeat(routed, parts, part, [mark(second, 10**9), w_a])
    wide = spread(wide, TENSOR)
    own, back, squares = pl.pallas_call(
        prefix_kernel,
        out_shape=[
            jax.ShapeDtypeStruct((length_p, 2 * HEAD_DIM), F32),
            jax.ShapeDtypeStruct((length_p, 2 * HEAD_DIM), BF16),
            jax.ShapeDtypeStruct((length_p // HEAD_DIM, HEAD_DIM), F32),
        ],
        in_specs=[smem(), vmem()] + [anywhere()] * 10,
        out_specs=[vmem()] * 3,
        scratch_shapes=[
            pltpu.VMEM((4, length_p, part), BF16),
            pltpu.VMEM((half, 4 * HEAD_DIM), BF16),
            pltpu.VMEM((length_p, 4 * HEAD_DIM), F32),
            pltpu.SemaphoreType.DMA((7,)),
            pltpu.SemaphoreType.DMA((4,)),
        ],
        compiler_params=params(18),
        cost_estimate=pl.CostEstimate(flops=2147483648, bytes_accessed=8 << 20, transcendentals=0),
        name="prefix_projection",
    )(place, gain, *[in_hbm(x) for x in [*blocks, w_key, w_value, w_a]])
    far, far_squares = swap(back, "xh"), swap(squares, "xh")

    q, k, v = pl.pallas_call(
        state_kernel,
        out_shape=[
            jax.ShapeDtypeStruct((rows, w_query.shape[1]), BF16),
            jax.ShapeDtypeStruct((rows, HEAD_DIM), BF16),
            jax.ShapeDtypeStruct((rows, HEAD_DIM), BF16),
        ],
        in_specs=[vmem()] * 2 + [anywhere()] * 3,
        out_specs=[vmem()] * 3,
        scratch_shapes=[
            pltpu.VMEM((parts * part, w_query.shape[1] + 2 * HEAD_DIM), BF16),
            pltpu.SemaphoreType.DMA((2, 3)),
        ],
        compiler_params=params(20),
        cost_estimate=pl.CostEstimate(flops=1610612736, bytes_accessed=8 << 20, transcendentals=0),
        name="state_projection",
    )(wide, gain, in_hbm(w_query), in_hbm(w_key), in_hbm(w_value))

    limit = lax.dynamic_index_in_dim(prefix_len, (xl * 8 + z) * 2 + c, keepdims=False)
    terms = pl.pallas_call(
        attention_kernel,
        out_shape=jax.ShapeDtypeStruct((parts, rows, part), BF16),
        in_specs=[smem()] + [vmem()] * 9,
        out_specs=vmem(),
        scratch_shapes=[
            pltpu.VMEM((rows, w_out.shape[0]), BF16),
            pltpu.VMEM((length_p + rows, 2 * HEAD_DIM), BF16),
        ],
        compiler_params=params(24),
        cost_estimate=pl.CostEstimate(flops=1800000000, bytes_accessed=8 << 20, transcendentals=1310720),
        name="attention",
    )(limit[None], q, own, in_vmem(far), in_vmem(squares), in_vmem(far_squares), k, v, routed[:, part:], w_out)

    mixed = jnp.sum(spread(terms, TENSOR).astype(F32), axis=0).astype(BF16)
    here = spread(mixed.reshape(chips, slots, piece, part), CHIPS)
    there = swap(here, "c")
    home = spread(select(outward, here, there), CHIPS)
    return home.transpose(1, 0, 2, 3).reshape(slots, length, part)


def solution(mesh):
    split = Mesh(mesh.devices.reshape(2, 8, 2, 2, 4), ("xl", "z", "c", "xh", "y"))
    placed = (
        P(PROMPT, None, TENSOR),
        P(PROMPT, None, TENSOR),
        P(),
        P(None, TENSOR),
        P(None, TENSOR),
        P(None, TENSOR),
        P(TENSOR, None),
        P(PROMPT, None),
        P(),
        P(PROMPT, None),
    )
    return jax.shard_map(
        per_device,
        mesh=split,
        in_specs=placed,
        out_specs=P(PROMPT, None, TENSOR),
        check_vma=False,
    )
```
